32 devices in a mesh: dp: 16 (over z, y, x), tensor: 2 (over core).
Axes of the slice: x: 2, y: 2, z: 4, core: 2. Of those that a mesh axis runs over, the one named last changes fastest.
Arguments:
- inputs: bfloat16 [22528, 512], P(('dp', 'tensor')), may hold values from -14 to 14
- cotangent: float32 [22528, 512], P(('dp', 'tensor')), may hold values from -8 to 8
- norm_gain: float32 [5, 512], replicated, may hold values from 0.5 to 1.5
- norm_shift: float32 [5, 512], replicated, may hold values from -1.5 to 1.5
- ff_in_weight: bfloat16 [2, 512, 2048], P(None, None, 'tensor'), may hold values from -0.25 to 0.25
- ff_in_bias: float32 [2, 2048], P(None, 'tensor'), may hold values from -3 to 3
- ff_out_weight: bfloat16 [2, 2048, 512], P(None, 'tensor'), may hold values from -0.125 to 0.125
- ff_out_bias: float32 [2, 512], replicated, may hold values from -3 to 3
- qkv_weight: bfloat16 [3, 512, 512], P(None, None, 'tensor'), may hold values from -0.25 to 0.25
- pos_weight: bfloat16 [512, 512], P(None, 'tensor'), may hold values from -0.25 to 0.25
- content_bias: float32 [512], P('tensor'), may hold values from -4 to 4
- position_bias: float32 [512], P('tensor'), may hold values from -4 to 4
- attn_out_weight: bfloat16 [512, 512], P('tensor'), may hold values from -1 to 1
- attn_out_bias: float32 [512], replicated, may hold values from -3 to 3
- glu_weight: bfloat16 [2, 512, 512], P(None, None, 'tensor'), may hold values from -0.25 to 0.25
- glu_bias: float32 [2, 512], P(None, 'tensor'), may hold values from -3 to 3
- depth_weight: float32 [31, 512], P(None, 'tensor'), may hold values from -1 to 1
- bn_gain: float32 [512], P('tensor'), may hold values from 0.5 to 1.5
- bn_shift: float32 [512], P('tensor'), may hold values from -3 to 3
- conv_out_weight: bfloat16 [512, 512], P('tensor'), may hold values from -0.25 to 0.25
- conv_out_bias: float32 [512], replicated, may hold values from -3 to 3
Outputs:
- result: float32 [22528, 512], P(('dp', 'tensor'))
- input_grad: float32 [22528, 512], P(('dp', 'tensor'))
- grad_norm_gain: float32 [5, 512], replicated
- grad_norm_shift: float32 [5, 512], replicated
- grad_ff_in_weight: float32 [2, 512, 2048], P(None, None, 'tensor')
- grad_ff_in_bias: float32 [2, 2048], P(None, 'tensor')
- grad_ff_out_weight: float32 [2, 2048, 512], P(None, 'tensor')
- grad_ff_out_bias: float32 [2, 512], replicated
- grad_qkv_weight: float32 [3, 512, 512], P(None, None, 'tensor')
- grad_pos_weight: float32 [512, 512], P(None, 'tensor')
- grad_content_bias: float32 [512], P('tensor')
- grad_position_bias: float32 [512], P('tensor')
- grad_attn_out_weight: float32 [512, 512], P('tensor')
- grad_attn_out_bias: float32 [512], replicated
- grad_glu_weight: float32 [2, 512, 512], P(None, None, 'tensor')
- grad_glu_bias: float32 [2, 512], P(None, 'tensor')
- grad_depth_weight: float32 [31, 512], P(None, 'tensor')
- grad_bn_gain: float32 [512], P('tensor')
- grad_bn_shift: float32 [512], P('tensor')
- grad_conv_out_weight: float32 [512, 512], P('tensor')
- grad_conv_out_bias: float32 [512], replicated
The draws below stay inside these ranges and needn't reach their ends.
All inputs are finite; a program needn't handle non-finite values.
Results may differ from the reference program's by a relative error of at most 0.038.
Values may be sent and summed in bfloat16 or wider, within the bound.
A program may use at most 192 MiB of HBM per device.

```python
import math
import jax
import jax.numpy as jnp
from jax import lax

D = 512
HEADS = 8
HEAD = 64
FF = 2048
KERNEL = 31
SEQ_LEN = 352
TOKENS = 22528


def sequence_level():
    seq_index = (jnp.arange(TOKENS) // SEQ_LEN).astype(jnp.float32)
    return seq_index / (TOKENS // SEQ_LEN)


def draw_inputs(key, part):
    key = jax.random.fold_in(key, 11)
    first_key, second_key = jax.random.split(key)
    direction = jnp.clip(jax.random.normal(second_key, (D,), jnp.float32), -3.0, 3.0)
    noise = jax.random.truncated_normal(first_key, -5.0, 5.0, (TOKENS, D), jnp.float32)
    lift = 2.0
    level = sequence_level()
    return (noise + lift * level[:, None] * direction[None, :]).astype(jnp.bfloat16)


def draw_cotangent(key, part):
    key = jax.random.fold_in(key, 23)
    first_key = jax.random.fold_in(key, 0)
    weight_rows = 0.5 + sequence_level()
    noise = jax.random.truncated_normal(first_key, -5.0, 5.0, (TOKENS, D), jnp.float32)
    return noise * weight_rows[:, None]


def steps_of(rng, dims, cuts, smallest, largest):
    loudness, own = 1.0, jax.random.fold_in(rng, 6)
    for axis_at, shards_of in cuts:
        heights = jnp.exp(jax.random.uniform(jax.random.fold_in(own, axis_at), (shards_of,), jnp.float32, smallest / len(cuts), largest / len(cuts)))
        loudness = loudness * jnp.repeat(heights, dims[axis_at] // shards_of).reshape([-1 if axis == axis_at else 1 for axis in range(len(dims))])
    return loudness


def normal_values(stream_key, dims, scale, most, cuts=(), dtype=jnp.bfloat16):
    entries = jax.random.normal(stream_key, dims, jnp.float32) * scale
    if len(cuts) > 0:
        entries = steps_of(stream_key, dims, cuts, -0.22, 0.18) * entries
    return jnp.clip(entries, min=-most, max=most).astype(dtype)


def setup_inputs(seed: int = 0) -> dict:
    key_list = jax.random.split(jax.random.key(seed), 22)
    inputs = draw_inputs(jax.random.fold_in(key_list[21], 71), 0)
    cotangent = draw_cotangent(jax.random.fold_in(key_list[21], 71), 0)
    norm_gain = jnp.clip(jax.random.uniform(key_list[2], (5, D), jnp.float32, 0.5, 1.5), 0.5, 1.5)
    norm_shift = normal_values(key_list[3], (5, D), 0.3, 1.5, (), jnp.float32)
    ff_in_weight = normal_values(key_list[4], (2, D, FF), D ** -0.5, 0.25, ((2, 2),))
    ff_in_bias = normal_values(key_list[5], (2, FF), 0.5, 3.0, ((1, 2),), jnp.float32)
    ff_out_weight = normal_values(key_list[6], (2, FF, D), FF ** -0.5, 0.125, ((1, 2),))
    ff_out_bias = normal_values(key_list[7], (2, D), 0.5, 3.0, (), jnp.float32)
    qkv_weight = normal_values(key_list[8], (3, D, D), D ** -0.5, 0.25, ((2, 2),))
    pos_weight = normal_values(key_list[9], (D, D), D ** -0.5, 0.25, ((1, 2),))
    content_bias = normal_values(key_list[10], (D,), 1.0, 4.0, ((0, 2),), jnp.float32)
    position_bias = normal_values(key_list[11], (D,), 1.0, 4.0, ((0, 2),), jnp.float32)
    attn_out_weight = normal_values(key_list[12], (D, D), (D // 16) ** -0.5, 1.0, ((0, 2),))
    attn_out_bias = normal_values(key_list[13], (D,), 0.5, 3.0, (), jnp.float32)
    glu_weight = normal_values(key_list[14], (2, D, D), D ** -0.5, 0.25, ((2, 2),))
    glu_bias = normal_values(key_list[15], (2, D), 0.5, 3.0, ((1, 2),), jnp.float32)
    depth_weight = normal_values(key_list[16], (KERNEL, D), KERNEL ** -0.5, 1.0, ((1, 2),), jnp.float32)
    bn_gain = jnp.clip(0.5 + 1.0 * jax.random.uniform(key_list[17], (D,), jnp.float32) ** steps_of(key_list[17], (D,), ((0, 2),), -0.2, 0.2), 0.5, 1.5)
    bn_shift = normal_values(key_list[18], (D,), 0.5, 3.0, ((0, 2),), jnp.float32)
    conv_out_weight = normal_values(key_list[19], (D, D), D ** -0.5, 0.25, ((0, 2),))
    conv_out_bias = normal_values(key_list[20], (D,), 0.5, 3.0, (), jnp.float32)
    return {"inputs": inputs, "cotangent": cotangent, "norm_gain": norm_gain, "norm_shift": norm_shift, "ff_in_weight": ff_in_weight, "ff_in_bias": ff_in_bias, "ff_out_weight": ff_out_weight, "ff_out_bias": ff_out_bias, "qkv_weight": qkv_weight, "pos_weight": pos_weight, "content_bias": content_bias, "position_bias": position_bias, "attn_out_weight": attn_out_weight, "attn_out_bias": attn_out_bias, "glu_weight": glu_weight, "glu_bias": glu_bias, "depth_weight": depth_weight, "bn_gain": bn_gain, "bn_shift": bn_shift, "conv_out_weight": conv_out_weight, "conv_out_bias": conv_out_bias}


@jax.custom_vjp
def low(v):
    return lax.optimization_barrier(v.astype(jnp.bfloat16)).astype(jnp.float32)

@jax.custom_vjp
def low_back(v):
    return v

def low_keep(v):
    return (low(v), None)

def low_pass(kept, grad):
    return (grad,)

def back_keep(v):
    return (v, None)

def back_low(kept, grad):
    return (low(grad),)
low.defvjp(low_keep, low_pass)
low_back.defvjp(back_keep, back_low)

def matmul(left, right):
    return jnp.dot(left, right, precision=lax.Precision.HIGHEST, preferred_element_type=jnp.float32)

def rounded_both(value):
    return low(low_back(value))

def layer_norm(stream, gain_row, offset):
    row_mean = lax.optimization_barrier(jnp.mean(stream, axis=-1, keepdims=True))
    centered = stream - row_mean
    variance = lax.optimization_barrier(jnp.mean(centered * centered, axis=-1, keepdims=True))
    return centered * lax.rsqrt(variance + 1e-05) * gain_row + offset

def position_table(length, width):
    distance = (length - 1 - jnp.arange(2 * length - 1)).astype(jnp.float32)
    frequency = jnp.exp(jnp.arange(0, width, 2).astype(jnp.float32) * (-math.log(10000.0) / width))
    angles = distance[:, None] * frequency[None, :]
    return jnp.stack([jnp.sin(angles), jnp.cos(angles)], axis=-1).reshape(2 * length - 1, width)

def shift_relative(full):
    length = full.shape[-2]
    leading = full.shape[:-2]
    flat_rows = full.reshape(leading + (length * (2 * length - 1),))
    flat_rows = lax.slice_in_dim(flat_rows, length - 1, length - 1 + length * (2 * length - 2), axis=flat_rows.ndim - 1)
    return flat_rows.reshape(leading + (length, 2 * length - 2))[..., :length]

def depthwise(blocks, kernel):
    half_width = kernel.shape[0] // 2
    length = blocks.shape[1]
    padded = jnp.pad(blocks, ((0, 0), (half_width, half_width), (0, 0)))
    total = jnp.zeros(blocks.shape, jnp.float32)
    for offset_tap in range(kernel.shape[0]):
        total = total + padded[:, offset_tap:offset_tap + length, :] * kernel[offset_tap]
    return total

def feed_forward(stream, gain_row, offset, weight_in, bias_in, weight_out, bias_out):
    normed = low(layer_norm(stream, gain_row, offset))
    preact = low_back(matmul(normed, weight_in)) + bias_in
    hidden = low(jax.nn.silu(preact))
    return stream + 0.5 * (low_back(matmul(hidden, weight_out)) + bias_out)

def attend_one(pieces, pos_keys):
    query_u, query_v, keys, values = pieces
    content = jnp.einsum('ihe,jhe->hij', query_u, keys, precision=lax.Precision.HIGHEST)
    relative = jnp.einsum('ihe,che->hic', query_v, pos_keys, precision=lax.Precision.HIGHEST)
    scores = low_back(content + shift_relative(relative))
    weights = low(jax.nn.softmax(scores / math.sqrt(HEAD), axis=-1))
    return rounded_both(jnp.einsum('hij,jhe->ihe', weights, values, precision=lax.Precision.HIGHEST))

def attention(stream, gain_row, offset, qkv_weight, pos_weight, content_bias, position_bias, out_weight, out_bias):
    normed = low(layer_norm(stream, gain_row, offset))
    projected = low_back(jnp.einsum('rd,kde->kre', normed, qkv_weight, precision=lax.Precision.HIGHEST))
    seq_shape = (TOKENS // SEQ_LEN, SEQ_LEN, HEADS, HEAD)
    query_u = low(projected[0] + content_bias).reshape(seq_shape)
    query_v = low(projected[0] + position_bias).reshape(seq_shape)
    keys = low(projected[1]).reshape(seq_shape)
    values = low(projected[2]).reshape(seq_shape)
    table = low(position_table(SEQ_LEN, D))
    pos_keys = rounded_both(matmul(table, pos_weight)).reshape(2 * SEQ_LEN - 1, HEADS, HEAD)

    def attend_block(pieces):
        return attend_one(pieces, pos_keys)
    context = lax.map(jax.checkpoint(attend_block), (query_u, query_v, keys, values))
    context = context.reshape(TOKENS, D)
    return stream + low_back(matmul(context, out_weight)) + out_bias

def convolution(stream, gain_row, offset, glu_weight, glu_bias, depth_weight, bn_gain, bn_shift, out_weight, out_bias):
    normed = low(layer_norm(stream, gain_row, offset))
    preact = low_back(jnp.einsum('rd,kde->kre', normed, glu_weight, precision=lax.Precision.HIGHEST)) + glu_bias[:, None, :]
    gated = preact[0] * jax.nn.sigmoid(preact[1])
    mixed = depthwise(gated.reshape(TOKENS // SEQ_LEN, SEQ_LEN, D), depth_weight).reshape(TOKENS, D)
    batch_mean = lax.optimization_barrier(jnp.mean(mixed, axis=0))
    variance = lax.optimization_barrier(jnp.mean(mixed * mixed, axis=0)) - batch_mean * batch_mean
    normal_bn = (mixed - batch_mean) * lax.rsqrt(variance + 1e-05) * bn_gain + bn_shift
    active = low(jax.nn.silu(normal_bn))
    return stream + low_back(matmul(active, out_weight)) + out_bias

def forward(inputs, norm_gain, norm_shift, ff_in_weight, ff_in_bias, ff_out_weight, ff_out_bias, qkv_weight, pos_weight, content_bias, position_bias, attn_out_weight, attn_out_bias, glu_weight, glu_bias, depth_weight, bn_gain, bn_shift, conv_out_weight, conv_out_bias):
    stream = feed_forward(inputs, norm_gain[0], norm_shift[0], ff_in_weight[0], ff_in_bias[0], ff_out_weight[0], ff_out_bias[0])
    stream = attention(stream, norm_gain[1], norm_shift[1], qkv_weight, pos_weight, content_bias, position_bias, attn_out_weight, attn_out_bias)
    stream = convolution(stream, norm_gain[2], norm_shift[2], glu_weight, glu_bias, depth_weight, bn_gain, bn_shift, conv_out_weight, conv_out_bias)
    stream = feed_forward(stream, norm_gain[3], norm_shift[3], ff_in_weight[1], ff_in_bias[1], ff_out_weight[1], ff_out_bias[1])
    return layer_norm(stream, norm_gain[4], norm_shift[4])

def reference(inputs, cotangent, norm_gain, norm_shift, ff_in_weight, ff_in_bias, ff_out_weight, ff_out_bias, qkv_weight, pos_weight, content_bias, position_bias, attn_out_weight, attn_out_bias, glu_weight, glu_bias, depth_weight, bn_gain, bn_shift, conv_out_weight, conv_out_bias):
    params = [inputs, norm_gain, norm_shift, ff_in_weight, ff_in_bias, ff_out_weight, ff_out_bias, qkv_weight, pos_weight, content_bias, position_bias, attn_out_weight, attn_out_bias, glu_weight, glu_bias, depth_weight, bn_gain, bn_shift, conv_out_weight, conv_out_bias]
    params = [value.astype(jnp.float32) for value in params]
    result, pullback = jax.vjp(forward, *params)
    input_grad, grad_norm_gain, grad_norm_shift, grad_ff_in_weight, grad_ff_in_bias, grad_ff_out_weight, grad_ff_out_bias, grad_qkv_weight, grad_pos_weight, grad_content_bias, grad_position_bias, grad_attn_out_weight, grad_attn_out_bias, grad_glu_weight, grad_glu_bias, grad_depth_weight, grad_bn_gain, grad_bn_shift, grad_conv_out_weight, grad_conv_out_bias = pullback(cotangent.astype(jnp.float32))
    return (result, input_grad, grad_norm_gain, grad_norm_shift, grad_ff_in_weight, grad_ff_in_bias, grad_ff_out_weight, grad_ff_out_bias, grad_qkv_weight, grad_pos_weight, grad_content_bias, grad_position_bias, grad_attn_out_weight, grad_attn_out_bias, grad_glu_weight, grad_glu_bias, grad_depth_weight, grad_bn_gain, grad_bn_shift, grad_conv_out_weight, grad_conv_out_bias)
```

```python
import functools
import math

import jax
import jax.numpy as jnp
from jax import lax
from jax.experimental import pallas as pl
from jax.experimental.pallas import tpu as pltpu
from jax.sharding import PartitionSpec as P

D = 512
HEAD = 64
SEQ_LEN = 352
POS_ROWS = 768
MESH = pl.DeviceIdType.MESH


def norm_forward(stream, gain_row, offset):
    row_mean = jnp.mean(stream, axis=-1, keepdims=True)
    centered = stream - row_mean
    inv_std = lax.rsqrt(jnp.mean(centered * centered, axis=-1, keepdims=True) + 1e-05)
    unit_rows = centered * inv_std
    return (unit_rows * gain_row + offset, unit_rows, inv_std)


def norm_backward(grad_rows, unit_rows, inv_std, gain_row):
    along = grad_rows * gain_row
    back_rows = inv_std * (
        along
        - jnp.mean(along, axis=-1, keepdims=True)
        - unit_rows * jnp.mean(along * unit_rows, axis=-1, keepdims=True)
    )
    return (back_rows, jnp.sum(grad_rows * unit_rows, axis=0), jnp.sum(grad_rows, axis=0))


def position_tables():
    column = jnp.arange(D)
    frequency = jnp.exp((2 * (column // 2)).astype(jnp.float32) * (-math.log(10000.0) / D))
    even = (column % 2) == 0
    coarse = (32 * jnp.arange(POS_ROWS // 32) - (SEQ_LEN - 1)).astype(jnp.float32)
    coarse = coarse[:, None] * frequency[None, :]
    fine = jnp.arange(32).astype(jnp.float32)[:, None] * frequency[None, :]
    sin_a, cos_a = jnp.sin(coarse), jnp.cos(coarse)
    first = jnp.where(even, sin_a, cos_a)
    second = jnp.where(even, cos_a, -sin_a)
    table = first[:, None, :] * jnp.cos(fine)[None] + second[:, None, :] * jnp.sin(fine)[None]
    flipped = table.reshape(POS_ROWS, D).astype(jnp.bfloat16)
    natural = jnp.where(even, -flipped, flipped)
    return (natural, flipped)


def depthwise(blocks, kernel):
    half_width = kernel.shape[0] // 2
    length = blocks.shape[1]
    padded = jnp.pad(blocks, ((0, 0), (half_width, half_width), (0, 0)))
    total = jnp.zeros(blocks.shape, jnp.float32)
    for offset_tap in range(kernel.shape[0]):
        total = total + padded[:, offset_tap : offset_tap + length, :] * kernel[offset_tap]
    return total


def depthwise_back(grad_blocks, blocks, kernel):
    taps = kernel.shape[0]
    half_width = taps // 2
    length = blocks.shape[1]
    padded_grad = jnp.pad(grad_blocks, ((0, 0), (half_width, half_width), (0, 0)))
    padded_in = jnp.pad(blocks, ((0, 0), (half_width, half_width), (0, 0)))
    d_input = jnp.zeros(blocks.shape, jnp.float32)
    tap_grads = []
    for offset_tap in range(taps):
        begin = 2 * half_width - offset_tap
        d_input = d_input + padded_grad[:, begin : begin + length, :] * kernel[offset_tap]
        tap_grads.append(
            jnp.sum(padded_in[:, offset_tap : offset_tap + length, :] * grad_blocks, axis=(0, 1))
        )
    return (d_input, jnp.stack(tap_grads))


def dot(left, right):
    return jnp.dot(left, right, preferred_element_type=jnp.float32)


def contract_first(left, right):
    return lax.dot_general(
        left, right, (((0,), (0,)), ((), ())), preferred_element_type=jnp.float32
    )


def contract_last(left, right):
    return lax.dot_general(
        left, right, (((1,), (1,)), ((), ())), preferred_element_type=jnp.float32
    )


def wide(value):
    return value.astype(jnp.float32)


def swap(value):
    return lax.ppermute(value, "tensor", [(0, 1), (1, 0)])


def add_up_group(mine, device_of, landed, send_sem, recv_sem):
    count = landed.shape[0]
    copies = []
    for away in range(1, count):
        copy = pltpu.make_async_remote_copy(
            src_ref=landed.at[mine],
            dst_ref=landed.at[mine],
            send_sem=send_sem.at[away],
            recv_sem=recv_sem.at[mine],
            device_id=device_of((mine + away) % count),
            device_id_type=MESH,
        )
        copy.start()
        copies.append(copy)
    for away in range(1, count):
        peer = (mine + away) % count
        pltpu.make_async_remote_copy(
            src_ref=landed.at[peer],
            dst_ref=landed.at[peer],
            send_sem=send_sem.at[away],
            recv_sem=recv_sem.at[peer],
            device_id=device_of(peer),
            device_id_type=MESH,
        ).wait_recv()
    for copy in copies:
        copy.wait_send()
    total = landed[0]
    for slot in range(1, count):
        total = total + landed[slot]
    return total


def sum_kernel(inner, outer, value_ref, *refs):
    out_ref, near, far, near_send, near_recv, far_send, far_recv = refs[-7:]
    me = lax.axis_index("dp")
    core = lax.axis_index("tensor")
    place, group = me % inner, me // inner

    def near_device(member):
        return (group * inner + member // 2, member % 2)

    def far_device(member):
        return (member * inner + place, core)

    near_mine = 2 * place + core
    barrier = pltpu.get_barrier_semaphore()
    for away in range(1, 2 * inner):
        partner = near_device((near_mine + away) % (2 * inner))
        pl.semaphore_signal(barrier, inc=1, device_id=partner, device_id_type=MESH)
    for away in range(1, outer):
        partner = far_device((group + away) % outer)
        pl.semaphore_signal(barrier, inc=1, device_id=partner, device_id_type=MESH)
    pl.semaphore_wait(barrier, 2 * inner + outer - 2)
    near[near_mine] = value_ref[...]
    far[group] = add_up_group(near_mine, near_device, near, near_send, near_recv)
    out_ref[...] = add_up_group(group, far_device, far, far_send, far_recv)


def sum_everywhere(value, collective_id, after=()):
    inner = 4
    outer = lax.axis_size("dp") // inner
    shape = value.shape
    return pl.pallas_call(
        functools.partial(sum_kernel, inner, outer),
        out_shape=jax.ShapeDtypeStruct(shape, jnp.float32),
        in_specs=[pl.BlockSpec(memory_space=pltpu.VMEM)]
        + [pl.BlockSpec(memory_space=pl.ANY)] * len(after),
        out_specs=pl.BlockSpec(memory_space=pltpu.VMEM),
        scratch_shapes=[
            pltpu.VMEM((2 * inner,) + shape, jnp.float32),
            pltpu.VMEM((outer,) + shape, jnp.float32),
            pltpu.SemaphoreType.DMA((2 * inner,)),
            pltpu.SemaphoreType.DMA((2 * inner,)),
            pltpu.SemaphoreType.DMA((outer,)),
            pltpu.SemaphoreType.DMA((outer,)),
        ],
        compiler_params=pltpu.CompilerParams(
            collective_id=collective_id, has_side_effects=True, vmem_limit_bytes=32 * 2**20
        ),
    )(value, *after)


def canonical(own, other):
    core = lax.axis_index("tensor")
    return jnp.where(
        core == 0,
        jnp.concatenate([own, other], axis=-1),
        jnp.concatenate([other, own], axis=-1),
    )


def halves(value):
    core = lax.axis_index("tensor")
    width = value.shape[-1] // 2
    low, high = value[..., :width], value[..., width:]
    return (jnp.where(core == 0, low, high), jnp.where(core == 0, high, low))


def attend_kernel(query_u, query_v, keys, values, pos_keys, context, probs):
    for head in range(2):
        cols = slice(HEAD * head, HEAD * (head + 1))
        content = contract_last(query_u[:, cols], keys[:, cols])
        relative = contract_last(query_v[:, cols], pos_keys[:, cols])
        relative = pltpu.roll(relative, POS_ROWS - (SEQ_LEN - 1), 1, stride=1, stride_axis=0)
        logits = (content + relative[:, :SEQ_LEN]) * (1.0 / math.sqrt(HEAD))
        powers = jnp.exp(logits - jnp.max(logits, axis=-1, keepdims=True))
        weights = powers * (1.0 / jnp.sum(powers, axis=-1, keepdims=True))
        low = weights.astype(jnp.bfloat16)
        probs[0, head] = low
        context[:, cols] = dot(low, values[:, cols]).astype(jnp.bfloat16)


def attend_back_kernel(
    d_context,
    query_u,
    query_v,
    keys,
    values,
    pos_keys,
    probs,
    mirror,
    *refs,
):
    d_query, d_keys, d_values, d_pos, bias_sums = refs[-5:]

    @pl.when(pl.program_id(1) == 0)
    def _():
        d_pos[...] = jnp.zeros_like(d_pos)
        bias_sums[...] = jnp.zeros_like(bias_sums)

    for head in range(2):
        cols = slice(HEAD * head, HEAD * (head + 1))
        low = probs[0, head]
        weights = low.astype(jnp.float32)
        grad = d_context[:, cols]
        d_values[:, cols] = contract_first(low, grad).astype(jnp.bfloat16)
        d_weights = contract_last(grad, values[:, cols])
        along = jnp.sum(d_weights * weights, axis=-1, keepdims=True)
        d_scores = (weights * (d_weights - along) * (1.0 / math.sqrt(HEAD))).astype(jnp.bfloat16)
        d_u = dot(d_scores, keys[:, cols])
        d_keys[:, cols] = contract_first(d_scores, query_u[:, cols]).astype(jnp.bfloat16)
        mirrored = dot(d_scores, mirror[...])
        d_relative = pltpu.roll(mirrored, 0, 1, stride=1, stride_axis=0).astype(jnp.bfloat16)
        d_v = dot(d_relative, pos_keys[:, cols])
        d_pos[:, cols] += contract_first(d_relative, query_v[:, cols])
        d_query[:, cols] = (d_u + d_v).astype(jnp.bfloat16)
        bias_sums[0:1, cols] += jnp.sum(d_u, axis=0, keepdims=True)
        bias_sums[1:2, cols] += jnp.sum(d_v, axis=0, keepdims=True)


def attend_specs():
    rows = pl.BlockSpec((SEQ_LEN, 2 * HEAD), lambda pair, seq: (seq, pair))
    pos = pl.BlockSpec((POS_ROWS, 2 * HEAD), lambda pair, seq: (0, pair))
    square = pl.BlockSpec((1, 2, SEQ_LEN, SEQ_LEN), lambda pair, seq: (seq, pair, 0, 0))
    return (rows, pos, square)


def attend(query_u, query_v, keys, values, pos_keys):
    row_count, width = keys.shape
    seqs, pairs = row_count // SEQ_LEN, width // (2 * HEAD)
    rows, pos, square = attend_specs()
    return pl.pallas_call(
        attend_kernel,
        grid=(pairs, seqs),
        in_specs=[rows, rows, rows, rows, pos],
        out_specs=[rows, square],
        out_shape=[
            jax.ShapeDtypeStruct((row_count, width), jnp.bfloat16),
            jax.ShapeDtypeStruct((seqs, 2 * pairs, SEQ_LEN, SEQ_LEN), jnp.bfloat16),
        ],
        compiler_params=pltpu.CompilerParams(vmem_limit_bytes=32 * 2**20),
        cost_estimate=pl.CostEstimate(
            flops=2 * seqs * pairs * 2 * SEQ_LEN * HEAD * (2 * SEQ_LEN + POS_ROWS),
            bytes_accessed=8 * 2**20,
            transcendentals=seqs * pairs * 2 * SEQ_LEN * SEQ_LEN,
        ),
    )(query_u, query_v, keys, values, pos_keys)


def attend_back(d_context, query_u, query_v, keys, values, pos_keys, probs, mirror, after=()):
    row_count, width = keys.shape
    seqs, pairs = row_count // SEQ_LEN, width // (2 * HEAD)
    rows, pos, square = attend_specs()
    whole = pl.BlockSpec((SEQ_LEN, POS_ROWS), lambda pair, seq: (0, 0))
    sums = pl.BlockSpec((8, 2 * HEAD), lambda pair, seq: (0, pair))
    low = jax.ShapeDtypeStruct((row_count, width), jnp.bfloat16)
    return pl.pallas_call(
        attend_back_kernel,
        grid=(pairs, seqs),
        in_specs=[rows, rows, rows, rows, rows, pos, square, whole]
        + [pl.BlockSpec(memory_space=pl.ANY)] * len(after),
        out_specs=[rows, rows, rows, pos, sums],
        out_shape=[
            low,
            low,
            low,
            jax.ShapeDtypeStruct((POS_ROWS, width), jnp.float32),
            jax.ShapeDtypeStruct((8, width), jnp.float32),
        ],
        compiler_params=pltpu.CompilerParams(vmem_limit_bytes=32 * 2**20),
        cost_estimate=pl.CostEstimate(
            flops=2 * seqs * pairs * 2 * SEQ_LEN * (4 * HEAD * SEQ_LEN + 3 * HEAD * POS_ROWS),
            bytes_accessed=8 * 2**20,
            transcendentals=0,
        ),
    )(d_context, query_u, query_v, keys, values, pos_keys, probs, mirror, *after)


def pair_sum(own_and_other):
    return [
        (own + swap(other.astype(jnp.bfloat16)).astype(jnp.float32)).astype(jnp.bfloat16)
        for own, other in own_and_other
    ]


def sum_in_turn(values, turn):
    count = lax.axis_size("dp")
    members = [2 * ((place + turn // 2) % count) for place in range(count)]
    groups = [members, [member + 1 for member in members]]
    if turn % 2:
        groups = groups[::-1]
    return lax.psum(tuple(values), ("dp", "tensor"), axis_index_groups=groups)


def ff_forward(stream, gain_row, offset, weights_in, biases_in, weights_out, bias_out):
    normed, unit_rows, inv_std = norm_forward(stream, gain_row, offset)
    normed = normed.astype(jnp.bfloat16)
    branch_out = 0.0
    preacts, hiddens = [], []
    for weight_in, bias_in, weight_out in zip(weights_in, biases_in, weights_out):
        preact = dot(normed, weight_in) + bias_in
        hidden = jax.nn.silu(preact).astype(jnp.bfloat16)
        branch_out = branch_out + dot(hidden, weight_out)
        preacts.append(preact)
        hiddens.append(hidden)
    return (
        stream + 0.5 * (branch_out + bias_out),
        (normed, unit_rows, inv_std, preacts, hiddens),
    )


def ff_backward(stream_grad, stored, gain_row, weights_in, weights_out, turn):
    normed, unit_rows, inv_std, preacts, hiddens = stored
    grad_out = (0.5 * stream_grad).astype(jnp.bfloat16)
    d_normed = 0.0
    grads_w_in, grads_b_in, grads_w_out = [], [], []
    for preact, hidden, weight_in, weight_out in zip(preacts, hiddens, weights_in, weights_out):
        grads_w_out.append(contract_first(hidden, grad_out))
        d_hidden = contract_last(grad_out, weight_out)
        gate_sig = jax.nn.sigmoid(preact)
        d_pre = d_hidden * gate_sig * (1.0 + preact * (1.0 - gate_sig))
        grads_b_in.append(jnp.sum(d_pre, axis=0))
        d_pre_low = d_pre.astype(jnp.bfloat16)
        grads_w_in.append(contract_first(normed, d_pre_low))
        d_normed = d_normed + contract_last(d_pre_low, weight_in)
    summed = sum_in_turn(pair_sum([grads_w_in, grads_w_out]), turn)
    d_stream, grad_gain, grad_shift = norm_backward(d_normed, unit_rows, inv_std, gain_row)
    return (
        stream_grad + d_stream,
        summed,
        grads_b_in,
        (0.5 * jnp.sum(stream_grad, axis=0), grad_gain, grad_shift),
    )


def attn_forward(
    stream, gain_row, offset, qkv_weights, pos_weights, content, position, out_weights, out_bias
):
    normed, unit_rows, inv_std = norm_forward(stream, gain_row, offset)
    normed = normed.astype(jnp.bfloat16)
    natural, flipped = position_tables()
    branch_out = 0.0
    kept = []
    for half in range(2):
        qkv = qkv_weights[half]
        query = dot(normed, qkv[0])
        query_u = (query + content[half]).astype(jnp.bfloat16)
        query_v = (query + position[half]).astype(jnp.bfloat16)
        keys = dot(normed, qkv[1]).astype(jnp.bfloat16)
        values = dot(normed, qkv[2]).astype(jnp.bfloat16)
        pos_keys = dot(natural, pos_weights[half]).astype(jnp.bfloat16)
        pos_flipped = dot(flipped, pos_weights[half]).astype(jnp.bfloat16)
        context, probs = attend(query_u, query_v, keys, values, pos_keys)
        branch_out = branch_out + dot(context, out_weights[half])
        kept.append((query_u, query_v, keys, values, pos_flipped, probs, context))
    return (stream + branch_out + out_bias, (normed, unit_rows, inv_std, flipped, kept))


def attn_backward(stream_grad, stored, gain_row, qkv_weights, out_weights, turn, earlier):
    normed, unit_rows, inv_std, table, kept = stored
    grad_out = stream_grad.astype(jnp.bfloat16)
    mirror = (
        lax.broadcasted_iota(jnp.int32, (SEQ_LEN, POS_ROWS), 0)
        + lax.broadcasted_iota(jnp.int32, (SEQ_LEN, POS_ROWS), 1)
        == SEQ_LEN - 1
    ).astype(jnp.bfloat16)
    d_normed = 0.0
    grads = []
    sums = []
    for half in range(2):
        query_u, query_v, keys, values, pos_flipped, probs, context = kept[half]
        grad_out_w = contract_first(context, grad_out)
        d_context = contract_last(grad_out, out_weights[half]).astype(jnp.bfloat16)
        d_query, d_keys, d_values, d_pos, bias_sums = attend_back(
            d_context,
            query_u,
            query_v,
            keys,
            values,
            pos_flipped,
            probs,
            mirror,
            (earlier[0],) if half == 1 else (),
        )
        parts = (d_query, d_keys, d_values)
        grad_qkv = jnp.stack([contract_first(normed, part) for part in parts])
        grad_pos = contract_first(table, d_pos.astype(jnp.bfloat16))
        for k, part in enumerate(parts):
            d_normed = d_normed + contract_last(part, qkv_weights[half][k])
        grads.append((grad_qkv, grad_pos, grad_out_w))
        sums.append(bias_sums[0:2])
    summed = sum_in_turn(pair_sum(list(zip(*grads))), turn)
    d_stream, grad_gain, grad_shift = norm_backward(d_normed, unit_rows, inv_std, gain_row)
    return (
        stream_grad + d_stream,
        summed,
        sums,
        (jnp.sum(stream_grad, axis=0), grad_gain, grad_shift),
    )


def conv_forward(
    stream,
    gain_row,
    offset,
    glu_weights,
    glu_biases,
    depth_weights,
    bn_gains,
    bn_shifts,
    out_weights,
    out_bias,
):
    row_count = stream.shape[0]
    normed, unit_rows, inv_std = norm_forward(stream, gain_row, offset)
    normed = normed.astype(jnp.bfloat16)
    kept, mixes, moments = [], [], []
    for half in range(2):
        value = dot(normed, glu_weights[half][0]) + glu_biases[half][0]
        gate_sig = jax.nn.sigmoid(dot(normed, glu_weights[half][1]) + glu_biases[half][1])
        blocks = (value * gate_sig).reshape(row_count // SEQ_LEN, SEQ_LEN, value.shape[1])
        mixed = depthwise(blocks, depth_weights[half]).reshape(value.shape)
        mixes.append(mixed)
        moments.append(jnp.stack([jnp.sum(mixed, axis=0), jnp.sum(mixed * mixed, axis=0)]))
        kept.append((value, gate_sig, blocks))
    sums = jnp.pad(canonical(*moments), ((0, 6), (0, 0)))
    sums = halves(sum_everywhere(sums, 1)[0:2])
    total_rows = row_count * lax.axis_size("dp") * lax.axis_size("tensor")
    branch_out = 0.0
    stored = []
    for half in range(2):
        batch_mean = sums[half][0] / total_rows
        bn_inv = lax.rsqrt(sums[half][1] / total_rows - batch_mean * batch_mean + 1e-05)
        unit_bn = (mixes[half] - batch_mean) * bn_inv
        normal_bn = unit_bn * bn_gains[half] + bn_shifts[half]
        active = jax.nn.silu(normal_bn).astype(jnp.bfloat16)
        branch_out = branch_out + dot(active, out_weights[half])
        stored.append(kept[half] + (unit_bn, normal_bn, bn_inv, active))
    return (stream + branch_out + out_bias, (normed, unit_rows, inv_std, stored))


def conv_backward(
    stream_grad, stored, gain_row, glu_weights, depth_weights, bn_gains, out_weights, turn
):
    normed, unit_rows, inv_std, kept = stored
    row_count = stream_grad.shape[0]
    grad_out = stream_grad.astype(jnp.bfloat16)
    d_normals, sums, grads_out_w = [], [], []
    for half in range(2):
        unit_bn, normal_bn, _, active = kept[half][3:]
        grads_out_w.append(contract_first(active, grad_out))
        d_active = contract_last(grad_out, out_weights[half])
        bn_sig = jax.nn.sigmoid(normal_bn)
        d_normal = d_active * bn_sig * (1.0 + normal_bn * (1.0 - bn_sig))
        d_normals.append(d_normal)
        sums.append(jnp.stack([jnp.sum(d_normal, axis=0), jnp.sum(d_normal * unit_bn, axis=0)]))
    totals = jnp.pad(canonical(*sums), ((0, 6), (0, 0)))
    totals = halves(sum_everywhere(totals, 2)[0:2])
    total_rows = row_count * lax.axis_size("dp") * lax.axis_size("tensor")
    d_normed = 0.0
    grads_glu, grads_b, grads_depth = [], [], []
    for half in range(2):
        value, gate_sig, blocks, unit_bn, _, bn_inv, _ = kept[half]
        d_mixed = (
            bn_gains[half]
            * bn_inv
            * (
                d_normals[half]
                - totals[half][0] / total_rows
                - unit_bn * (totals[half][1] / total_rows)
            )
        )
        d_gated, grad_depth = depthwise_back(
            d_mixed.reshape(blocks.shape), blocks, depth_weights[half]
        )
        d_gated = d_gated.reshape(d_mixed.shape)
        d_pres = (d_gated * gate_sig, d_gated * value * gate_sig * (1.0 - gate_sig))
        grads_b.append(jnp.stack([jnp.sum(d_pre, axis=0) for d_pre in d_pres]))
        lows = [d_pre.astype(jnp.bfloat16) for d_pre in d_pres]
        grads_glu.append(jnp.stack([contract_first(normed, low) for low in lows]))
        for k, low in enumerate(lows):
            d_normed = d_normed + contract_last(low, glu_weights[half][k])
        grads_depth.append(grad_depth)
    summed = sum_in_turn(pair_sum([grads_glu, grads_out_w]), turn)
    d_stream, grad_gain, grad_shift = norm_backward(d_normed, unit_rows, inv_std, gain_row)
    return (
        stream_grad + d_stream,
        summed,
        (grads_b, grads_depth),
        (jnp.sum(stream_grad, axis=0), grad_gain, grad_shift),
        totals[0],
    )


def shards(
    inputs,
    cotangent,
    norm_gain,
    norm_shift,
    ff_in_weight,
    ff_in_bias,
    ff_out_weight,
    ff_out_bias,
    qkv_weight,
    pos_weight,
    content_bias,
    position_bias,
    attn_out_weight,
    attn_out_bias,
    glu_weight,
    glu_bias,
    depth_weight,
    bn_gain,
    bn_shift,
    conv_out_weight,
    conv_out_bias,
):
    width = bn_gain.shape[0]
    ff_rows = ff_in_bias.shape[1] // width
    small = jnp.concatenate(
        [
            ff_in_bias.reshape(2 * ff_rows, width),
            content_bias[None],
            position_bias[None],
            glu_bias,
            bn_gain[None],
            bn_shift[None],
            depth_weight,
        ],
        axis=0,
    )
    other = swap(small)
    at = 2 * ff_rows
    ff_in_biases = [
        (ff_in_bias[f], other[f * ff_rows : (f + 1) * ff_rows].reshape(-1)) for f in range(2)
    ]
    content = (content_bias, other[at])
    position = (position_bias, other[at + 1])
    glu_biases = (glu_bias, other[at + 2 : at + 4])
    bn_gains = (bn_gain, other[at + 4])
    bn_shifts = (bn_shift, other[at + 5])
    depth_weights = (depth_weight, other[at + 6 :])

    other_in, other_out = swap(ff_in_weight), swap(ff_out_weight)
    ff_in = [(ff_in_weight[f], other_in[f]) for f in range(2)]
    ff_out = [(ff_out_weight[f], other_out[f]) for f in range(2)]
    qkv = (qkv_weight, swap(qkv_weight))
    pos = (pos_weight, swap(pos_weight))
    attn_out = (attn_out_weight, swap(attn_out_weight))
    glu = (glu_weight, swap(glu_weight))
    conv_out = (conv_out_weight, swap(conv_out_weight))

    stream = inputs.astype(jnp.float32)
    stream, first_saved = ff_forward(
        stream, norm_gain[0], norm_shift[0], ff_in[0], ff_in_biases[0], ff_out[0], ff_out_bias[0]
    )
    stream, attn_saved = attn_forward(
        stream, norm_gain[1], norm_shift[1], qkv, pos, content, position, attn_out, attn_out_bias
    )
    stream, conv_saved = conv_forward(
        stream,
        norm_gain[2],
        norm_shift[2],
        glu,
        glu_biases,
        depth_weights,
        bn_gains,
        bn_shifts,
        conv_out,
        conv_out_bias,
    )
    stream, second_saved = ff_forward(
        stream, norm_gain[3], norm_shift[3], ff_in[1], ff_in_biases[1], ff_out[1], ff_out_bias[1]
    )
    result, final_unit, final_inv = norm_forward(stream, norm_gain[4], norm_shift[4])
    grad, final_gain, final_shift = norm_backward(cotangent, final_unit, final_inv, norm_gain[4])
    grad, second_sum, second_bias, second_rows = ff_backward(
        grad, second_saved, norm_gain[3], ff_in[1], ff_out[1], 0
    )
    grad, conv_sum, conv_small, conv_rows, bn_totals = conv_backward(
        grad, conv_saved, norm_gain[2], glu, depth_weights, bn_gains, conv_out, 1
    )
    grad, attn_sum, attn_small, attn_rows = attn_backward(
        grad, attn_saved, norm_gain[1], qkv, attn_out, 2, second_sum
    )
    grad, first_sum, first_bias, first_rows = ff_backward(
        grad, first_saved, norm_gain[0], ff_in[0], ff_out[0], 3
    )

    shared = jnp.stack(
        [first_rows[1], attn_rows[1], conv_rows[1], second_rows[1], final_gain]
        + [first_rows[2], attn_rows[2], conv_rows[2], second_rows[2], final_shift]
        + [first_rows[0], second_rows[0], attn_rows[0], conv_rows[0]]
    )
    split = [
        jnp.concatenate(
            [
                first_bias[half].reshape(ff_rows, width),
                second_bias[half].reshape(ff_rows, width),
                attn_small[half],
                conv_small[0][half],
                conv_small[1][half],
            ],
            axis=0,
        )
        for half in range(2)
    ]
    packed = jnp.concatenate([shared, canonical(*split)], axis=0)
    rows = packed.shape[0]
    packed = jnp.pad(packed, ((0, -rows % 8), (0, 0)))
    packed = sum_everywhere(packed, 3, (conv_sum[0], attn_sum[0]))
    own = halves(packed[14:rows])[0]
    return (
        result,
        grad,
        packed[0:5],
        packed[5:10],
        wide(jnp.stack([first_sum[0], second_sum[0]])),
        own[0 : 2 * ff_rows].reshape(2, ff_rows * width),
        wide(jnp.stack([first_sum[1], second_sum[1]])),
        packed[10:12],
        wide(attn_sum[0]),
        wide(attn_sum[1]),
        own[2 * ff_rows],
        own[2 * ff_rows + 1],
        wide(attn_sum[2]),
        packed[12],
        wide(conv_sum[0]),
        own[2 * ff_rows + 2 : 2 * ff_rows + 4],
        own[2 * ff_rows + 4 :],
        bn_totals[1],
        bn_totals[0],
        wide(conv_sum[1]),
        packed[13],
    )


def solution(mesh):
    in_specs = (
        P(("dp", "tensor"), None),
        P(("dp", "tensor"), None),
        P(),
        P(),
        P(None, None, "tensor"),
        P(None, "tensor"),
        P(None, "tensor", None),
        P(),
        P(None, None, "tensor"),
        P(None, "tensor"),
        P("tensor"),
        P("tensor"),
        P("tensor", None),
        P(),
        P(None, None, "tensor"),
        P(None, "tensor"),
        P(None, "tensor"),
        P("tensor"),
        P("tensor"),
        P("tensor", None),
        P(),
    )
    out_specs = (
        P(("dp", "tensor"), None),
        P(("dp", "tensor"), None),
        P(),
        P(),
        P(None, None, "tensor"),
        P(None, "tensor"),
        P(None, "tensor", None),
        P(),
        P(None, None, "tensor"),
        P(None, "tensor"),
        P("tensor"),
        P("tensor"),
        P("tensor", None),
        P(),
        P(None, None, "tensor"),
        P(None, "tensor"),
        P(None, "tensor"),
        P("tensor"),
        P("tensor"),
        P("tensor", None),
        P(),
    )
    return jax.shard_map(shards, mesh=mesh, in_specs=in_specs, out_specs=out_specs, check_vma=False)
```

```python
import functools
import math

import jax
import jax.numpy as jnp
from jax import lax
from jax.experimental import pallas as pl
from jax.experimental.pallas import tpu as pltpu
from jax.sharding import PartitionSpec as P

D = 512
HEAD = 64
SEQ_LEN = 352
POS_ROWS = 768
MESH = pl.DeviceIdType.MESH


def norm_forward(stream, gain_row, offset):
    row_mean = jnp.mean(stream, axis=-1, keepdims=True)
    centered = stream - row_mean
    inv_std = lax.rsqrt(jnp.mean(centered * centered, axis=-1, keepdims=True) + 1e-05)
    unit_rows = centered * inv_std
    return (unit_rows * gain_row + offset, unit_rows, inv_std)


def norm_backward(grad_rows, unit_rows, inv_std, gain_row):
    along = grad_rows * gain_row
    back_rows = inv_std * (
        along
        - jnp.mean(along, axis=-1, keepdims=True)
        - unit_rows * jnp.mean(along * unit_rows, axis=-1, keepdims=True)
    )
    return (back_rows, jnp.sum(grad_rows * unit_rows, axis=0), jnp.sum(grad_rows, axis=0))


def position_tables():
    column = jnp.arange(D)
    frequency = jnp.exp((2 * (column // 2)).astype(jnp.float32) * (-math.log(10000.0) / D))
    even = (column % 2) == 0
    coarse = (32 * jnp.arange(POS_ROWS // 32) - (SEQ_LEN - 1)).astype(jnp.float32)
    coarse = coarse[:, None] * frequency[None, :]
    fine = jnp.arange(32).astype(jnp.float32)[:, None] * frequency[None, :]
    sin_a, cos_a = jnp.sin(coarse), jnp.cos(coarse)
    first = jnp.where(even, sin_a, cos_a)
    second = jnp.where(even, cos_a, -sin_a)
    table = first[:, None, :] * jnp.cos(fine)[None] + second[:, None, :] * jnp.sin(fine)[None]
    flipped = table.reshape(POS_ROWS, D).astype(jnp.bfloat16)
    natural = jnp.where(even, -flipped, flipped)
    return (natural, flipped)


def depthwise(blocks, kernel):
    half_width = kernel.shape[0] // 2
    length = blocks.shape[1]
    padded = jnp.pad(blocks, ((0, 0), (half_width, half_width), (0, 0)))
    total = jnp.zeros(blocks.shape, jnp.float32)
    for offset_tap in range(kernel.shape[0]):
        total = total + padded[:, offset_tap : offset_tap + length, :] * kernel[offset_tap]
    return total


def depthwise_back(grad_blocks, blocks, kernel):
    taps = kernel.shape[0]
    half_width = taps // 2
    length = blocks.shape[1]
    padded_grad = jnp.pad(grad_blocks, ((0, 0), (half_width, half_width), (0, 0)))
    padded_in = jnp.pad(blocks, ((0, 0), (half_width, half_width), (0, 0)))
    d_input = jnp.zeros(blocks.shape, jnp.float32)
    tap_grads = []
    for offset_tap in range(taps):
        begin = 2 * half_width - offset_tap
        d_input = d_input + padded_grad[:, begin : begin + length, :] * kernel[offset_tap]
        tap_grads.append(
            jnp.sum(padded_in[:, offset_tap : offset_tap + length, :] * grad_blocks, axis=(0, 1))
        )
    return (d_input, jnp.stack(tap_grads))


def dot(left, right):
    return jnp.dot(left, right, preferred_element_type=jnp.float32)


def contract_first(left, right):
    return lax.dot_general(
        left, right, (((0,), (0,)), ((), ())), preferred_element_type=jnp.float32
    )


def contract_last(left, right):
    return lax.dot_general(
        left, right, (((1,), (1,)), ((), ())), preferred_element_type=jnp.float32
    )


def wide(value):
    return value.astype(jnp.float32)


def swap(value):
    return lax.ppermute(value, "tensor", [(0, 1), (1, 0)])


def add_up_group(mine, device_of, landed, send_sem, recv_sem):
    count = landed.shape[0]
    copies = []
    for away in range(1, count):
        copy = pltpu.make_async_remote_copy(
            src_ref=landed.at[mine],
            dst_ref=landed.at[mine],
            send_sem=send_sem.at[away],
            recv_sem=recv_sem.at[mine],
            device_id=device_of((mine + away) % count),
            device_id_type=MESH,
        )
        copy.start()
        copies.append(copy)
    for away in range(1, count):
        peer = (mine + away) % count
        pltpu.make_async_remote_copy(
            src_ref=landed.at[peer],
            dst_ref=landed.at[peer],
            send_sem=send_sem.at[away],
            recv_sem=recv_sem.at[peer],
            device_id=device_of(peer),
            device_id_type=MESH,
        ).wait_recv()
    for copy in copies:
        copy.wait_send()
    total = landed[0]
    for slot in range(1, count):
        total = total + landed[slot]
    return total


def sum_kernel(inner, outer, value_ref, *refs):
    out_ref, near, far, near_send, near_recv, far_send, far_recv = refs[-7:]
    me = lax.axis_index("dp")
    core = lax.axis_index("tensor")
    place, group = me % inner, me // inner

    def near_device(member):
        return (group * inner + member // 2, member % 2)

    def far_device(member):
        return (member * inner + place, core)

    near_mine = 2 * place + core
    barrier = pltpu.get_barrier_semaphore()
    for away in range(1, 2 * inner):
        partner = near_device((near_mine + away) % (2 * inner))
        pl.semaphore_signal(barrier, inc=1, device_id=partner, device_id_type=MESH)
    for away in range(1, outer):
        partner = far_device((group + away) % outer)
        pl.semaphore_signal(barrier, inc=1, device_id=partner, device_id_type=MESH)
    pl.semaphore_wait(barrier, 2 * inner + outer - 2)
    near[near_mine] = value_ref[...]
    far[group] = add_up_group(near_mine, near_device, near, near_send, near_recv)
    out_ref[...] = add_up_group(group, far_device, far, far_send, far_recv)


def sum_everywhere(value, collective_id, after=()):
    inner = 4
    outer = lax.axis_size("dp") // inner
    shape = value.shape
    return pl.pallas_call(
        functools.partial(sum_kernel, inner, outer),
        out_shape=jax.ShapeDtypeStruct(shape, jnp.float32),
        in_specs=[pl.BlockSpec(memory_space=pltpu.VMEM)]
        + [pl.BlockSpec(memory_space=pl.ANY)] * len(after),
        out_specs=pl.BlockSpec(memory_space=pltpu.VMEM),
        scratch_shapes=[
            pltpu.VMEM((2 * inner,) + shape, jnp.float32),
            pltpu.VMEM((outer,) + shape, jnp.float32),
            pltpu.SemaphoreType.DMA((2 * inner,)),
            pltpu.SemaphoreType.DMA((2 * inner,)),
            pltpu.SemaphoreType.DMA((outer,)),
            pltpu.SemaphoreType.DMA((outer,)),
        ],
        compiler_params=pltpu.CompilerParams(
            collective_id=collective_id, has_side_effects=True, vmem_limit_bytes=32 * 2**20
        ),
    )(value, *after)


def canonical(own, other):
    core = lax.axis_index("tensor")
    return jnp.where(
        core == 0,
        jnp.concatenate([own, other], axis=-1),
        jnp.concatenate([other, own], axis=-1),
    )


def halves(value):
    core = lax.axis_index("tensor")
    width = value.shape[-1] // 2
    low, high = value[..., :width], value[..., width:]
    return (jnp.where(core == 0, low, high), jnp.where(core == 0, high, low))


def attend_kernel(query_u, query_v, keys, values, pos_keys, context, probs):
    for head in range(2):
        cols = slice(HEAD * head, HEAD * (head + 1))
        content = contract_last(query_u[:, cols], keys[:, cols])
        relative = contract_last(query_v[:, cols], pos_keys[:, cols])
        relative = pltpu.roll(relative, POS_ROWS - (SEQ_LEN - 1), 1, stride=1, stride_axis=0)
        logits = (content + relative[:, :SEQ_LEN]) * (1.0 / math.sqrt(HEAD))
        powers = jnp.exp(logits - jnp.max(logits, axis=-1, keepdims=True))
        weights = powers * (1.0 / jnp.sum(powers, axis=-1, keepdims=True))
        low = weights.astype(jnp.bfloat16)
        probs[0, head] = low
        context[:, cols] = dot(low, values[:, cols]).astype(jnp.bfloat16)


def attend_back_kernel(
    d_context,
    query_u,
    query_v,
    keys,
    values,
    pos_keys,
    probs,
    mirror,
    *refs,
):
    d_query, d_keys, d_values, d_pos, bias_sums = refs[-5:]

    @pl.when(pl.program_id(1) == 0)
    def _():
        d_pos[...] = jnp.zeros_like(d_pos)
        bias_sums[...] = jnp.zeros_like(bias_sums)

    for head in range(2):
        cols = slice(HEAD * head, HEAD * (head + 1))
        low = probs[0, head]
        weights = low.astype(jnp.float32)
        grad = d_context[:, cols]
        d_values[:, cols] = contract_first(low, grad).astype(jnp.bfloat16)
        d_weights = contract_last(grad, values[:, cols])
        along = jnp.sum(d_weights * weights, axis=-1, keepdims=True)
        d_scores = (weights * (d_weights - along) * (1.0 / math.sqrt(HEAD))).astype(jnp.bfloat16)
        d_u = dot(d_scores, keys[:, cols])
        d_keys[:, cols] = contract_first(d_scores, query_u[:, cols]).astype(jnp.bfloat16)
        mirrored = dot(d_scores, mirror[...])
        d_relative = pltpu.roll(mirrored, 0, 1, stride=1, stride_axis=0).astype(jnp.bfloat16)
        d_v = dot(d_relative, pos_keys[:, cols])
        d_pos[:, cols] += contract_first(d_relative, query_v[:, cols])
        d_query[:, cols] = (d_u + d_v).astype(jnp.bfloat16)
        bias_sums[0:1, cols] += jnp.sum(d_u, axis=0, keepdims=True)
        bias_sums[1:2, cols] += jnp.sum(d_v, axis=0, keepdims=True)


def attend_specs():
    rows = pl.BlockSpec((SEQ_LEN, 2 * HEAD), lambda pair, seq: (seq, pair))
    pos = pl.BlockSpec((POS_ROWS, 2 * HEAD), lambda pair, seq: (0, pair))
    square = pl.BlockSpec((1, 2, SEQ_LEN, SEQ_LEN), lambda pair, seq: (seq, pair, 0, 0))
    return (rows, pos, square)


def attend(query_u, query_v, keys, values, pos_keys):
    row_count, width = keys.shape
    seqs, pairs = row_count // SEQ_LEN, width // (2 * HEAD)
    rows, pos, square = attend_specs()
    return pl.pallas_call(
        attend_kernel,
        grid=(pairs, seqs),
        in_specs=[rows, rows, rows, rows, pos],
        out_specs=[rows, square],
        out_shape=[
            jax.ShapeDtypeStruct((row_count, width), jnp.bfloat16),
            jax.ShapeDtypeStruct((seqs, 2 * pairs, SEQ_LEN, SEQ_LEN), jnp.bfloat16),
        ],
        compiler_params=pltpu.CompilerParams(vmem_limit_bytes=32 * 2**20),
        cost_estimate=pl.CostEstimate(
            flops=2 * seqs * pairs * 2 * SEQ_LEN * HEAD * (2 * SEQ_LEN + POS_ROWS),
            bytes_accessed=8 * 2**20,
            transcendentals=seqs * pairs * 2 * SEQ_LEN * SEQ_LEN,
        ),
    )(query_u, query_v, keys, values, pos_keys)


def attend_back(d_context, query_u, query_v, keys, values, pos_keys, probs, mirror, after=()):
    row_count, width = keys.shape
    seqs, pairs = row_count // SEQ_LEN, width // (2 * HEAD)
    rows, pos, square = attend_specs()
    whole = pl.BlockSpec((SEQ_LEN, POS_ROWS), lambda pair, seq: (0, 0))
    sums = pl.BlockSpec((8, 2 * HEAD), lambda pair, seq: (0, pair))
    low = jax.ShapeDtypeStruct((row_count, width), jnp.bfloat16)
    return pl.pallas_call(
        attend_back_kernel,
        grid=(pairs, seqs),
        in_specs=[rows, rows, rows, rows, rows, pos, square, whole]
        + [pl.BlockSpec(memory_space=pl.ANY)] * len(after),
        out_specs=[rows, rows, rows, pos, sums],
        out_shape=[
            low,
            low,
            low,
            jax.ShapeDtypeStruct((POS_ROWS, width), jnp.float32),
            jax.ShapeDtypeStruct((8, width), jnp.float32),
        ],
        compiler_params=pltpu.CompilerParams(vmem_limit_bytes=32 * 2**20),
        cost_estimate=pl.CostEstimate(
            flops=2 * seqs * pairs * 2 * SEQ_LEN * (4 * HEAD * SEQ_LEN + 3 * HEAD * POS_ROWS),
            bytes_accessed=8 * 2**20,
            transcendentals=0,
        ),
    )(d_context, query_u, query_v, keys, values, pos_keys, probs, mirror, *after)


def pair_sum(own_and_other):
    return [
        (own + swap(other.astype(jnp.bfloat16)).astype(jnp.float32)).astype(jnp.bfloat16)
        for own, other in own_and_other
    ]


def sum_in_turn(values, turn):
    return lax.psum(tuple(values), "dp")


def ff_forward(stream, gain_row, offset, weights_in, biases_in, weights_out, bias_out):
    normed, unit_rows, inv_std = norm_forward(stream, gain_row, offset)
    normed = normed.astype(jnp.bfloat16)
    branch_out = 0.0
    preacts, hiddens = [], []
    for weight_in, bias_in, weight_out in zip(weights_in, biases_in, weights_out):
        preact = dot(normed, weight_in) + bias_in
        hidden = jax.nn.silu(preact).astype(jnp.bfloat16)
        branch_out = branch_out + dot(hidden, weight_out)
        preacts.append(preact)
        hiddens.append(hidden)
    return (
        stream + 0.5 * (branch_out + bias_out),
        (normed, unit_rows, inv_std, preacts, hiddens),
    )


def ff_backward(stream_grad, stored, gain_row, weights_in, weights_out, turn):
    normed, unit_rows, inv_std, preacts, hiddens = stored
    grad_out = (0.5 * stream_grad).astype(jnp.bfloat16)
    d_normed = 0.0
    grads_w_in, grads_b_in, grads_w_out = [], [], []
    for preact, hidden, weight_in, weight_out in zip(preacts, hiddens, weights_in, weights_out):
        grads_w_out.append(contract_first(hidden, grad_out))
        d_hidden = contract_last(grad_out, weight_out)
        gate_sig = jax.nn.sigmoid(preact)
        d_pre = d_hidden * gate_sig * (1.0 + preact * (1.0 - gate_sig))
        grads_b_in.append(jnp.sum(d_pre, axis=0))
        d_pre_low = d_pre.astype(jnp.bfloat16)
        grads_w_in.append(contract_first(normed, d_pre_low))
        d_normed = d_normed + contract_last(d_pre_low, weight_in)
    summed = sum_in_turn(pair_sum([grads_w_in, grads_w_out]), turn)
    d_stream, grad_gain, grad_shift = norm_backward(d_normed, unit_rows, inv_std, gain_row)
    return (
        stream_grad + d_stream,
        summed,
        grads_b_in,
        (0.5 * jnp.sum(stream_grad, axis=0), grad_gain, grad_shift),
    )


def attn_forward(
    stream, gain_row, offset, qkv_weights, pos_weights, content, position, out_weights, out_bias
):
    normed, unit_rows, inv_std = norm_forward(stream, gain_row, offset)
    normed = normed.astype(jnp.bfloat16)
    natural, flipped = position_tables()
    branch_out = 0.0
    kept = []
    for half in range(2):
        qkv = qkv_weights[half]
        query = dot(normed, qkv[0])
        query_u = (query + content[half]).astype(jnp.bfloat16)
        query_v = (query + position[half]).astype(jnp.bfloat16)
        keys = dot(normed, qkv[1]).astype(jnp.bfloat16)
        values = dot(normed, qkv[2]).astype(jnp.bfloat16)
        pos_keys = dot(natural, pos_weights[half]).astype(jnp.bfloat16)
        pos_flipped = dot(flipped, pos_weights[half]).astype(jnp.bfloat16)
        context, probs = attend(query_u, query_v, keys, values, pos_keys)
        branch_out = branch_out + dot(context, out_weights[half])
        kept.append((query_u, query_v, keys, values, pos_flipped, probs, context))
    return (stream + branch_out + out_bias, (normed, unit_rows, inv_std, flipped, kept))


def attn_backward(stream_grad, stored, gain_row, qkv_weights, out_weights, turn, earlier):
    normed, unit_rows, inv_std, table, kept = stored
    grad_out = stream_grad.astype(jnp.bfloat16)
    mirror = (
        lax.broadcasted_iota(jnp.int32, (SEQ_LEN, POS_ROWS), 0)
        + lax.broadcasted_iota(jnp.int32, (SEQ_LEN, POS_ROWS), 1)
        == SEQ_LEN - 1
    ).astype(jnp.bfloat16)
    d_normed = 0.0
    grads = []
    sums = []
    for half in range(2):
        query_u, query_v, keys, values, pos_flipped, probs, context = kept[half]
        grad_out_w = contract_first(context, grad_out)
        d_context = contract_last(grad_out, out_weights[half]).astype(jnp.bfloat16)
        d_query, d_keys, d_values, d_pos, bias_sums = attend_back(
            d_context,
            query_u,
            query_v,
            keys,
            values,
            pos_flipped,
            probs,
            mirror,
            (),
        )
        parts = (d_query, d_keys, d_values)
        grad_qkv = jnp.stack([contract_first(normed, part) for part in parts])
        grad_pos = contract_first(table, d_pos.astype(jnp.bfloat16))
        for k, part in enumerate(parts):
            d_normed = d_normed + contract_last(part, qkv_weights[half][k])
        grads.append((grad_qkv, grad_pos, grad_out_w))
        sums.append(bias_sums[0:2])
    summed = sum_in_turn(pair_sum(list(zip(*grads))), turn)
    d_stream, grad_gain, grad_shift = norm_backward(d_normed, unit_rows, inv_std, gain_row)
    return (
        stream_grad + d_stream,
        summed,
        sums,
        (jnp.sum(stream_grad, axis=0), grad_gain, grad_shift),
    )


def conv_forward(
    stream,
    gain_row,
    offset,
    glu_weights,
    glu_biases,
    depth_weights,
    bn_gains,
    bn_shifts,
    out_weights,
    out_bias,
):
    row_count = stream.shape[0]
    normed, unit_rows, inv_std = norm_forward(stream, gain_row, offset)
    normed = normed.astype(jnp.bfloat16)
    kept, mixes, moments = [], [], []
    for half in range(2):
        value = dot(normed, glu_weights[half][0]) + glu_biases[half][0]
        gate_sig = jax.nn.sigmoid(dot(normed, glu_weights[half][1]) + glu_biases[half][1])
        blocks = (value * gate_sig).reshape(row_count // SEQ_LEN, SEQ_LEN, value.shape[1])
        mixed = depthwise(blocks, depth_weights[half]).reshape(value.shape)
        mixes.append(mixed)
        moments.append(jnp.stack([jnp.sum(mixed, axis=0), jnp.sum(mixed * mixed, axis=0)]))
        kept.append((value, gate_sig, blocks))
    sums = jnp.pad(canonical(*moments), ((0, 6), (0, 0)))
    sums = halves(sum_everywhere(sums, 1)[0:2])
    total_rows = row_count * lax.axis_size("dp") * lax.axis_size("tensor")
    branch_out = 0.0
    stored = []
    for half in range(2):
        batch_mean = sums[half][0] / total_rows
        bn_inv = lax.rsqrt(sums[half][1] / total_rows - batch_mean * batch_mean + 1e-05)
        unit_bn = (mixes[half] - batch_mean) * bn_inv
        normal_bn = unit_bn * bn_gains[half] + bn_shifts[half]
        active = jax.nn.silu(normal_bn).astype(jnp.bfloat16)
        branch_out = branch_out + dot(active, out_weights[half])
        stored.append(kept[half] + (unit_bn, normal_bn, bn_inv, active))
    return (stream + branch_out + out_bias, (normed, unit_rows, inv_std, stored))


def conv_backward(
    stream_grad, stored, gain_row, glu_weights, depth_weights, bn_gains, out_weights, turn
):
    normed, unit_rows, inv_std, kept = stored
    row_count = stream_grad.shape[0]
    grad_out = stream_grad.astype(jnp.bfloat16)
    d_normals, sums, grads_out_w = [], [], []
    for half in range(2):
        unit_bn, normal_bn, _, active = kept[half][3:]
        grads_out_w.append(contract_first(active, grad_out))
        d_active = contract_last(grad_out, out_weights[half])
        bn_sig = jax.nn.sigmoid(normal_bn)
        d_normal = d_active * bn_sig * (1.0 + normal_bn * (1.0 - bn_sig))
        d_normals.append(d_normal)
        sums.append(jnp.stack([jnp.sum(d_normal, axis=0), jnp.sum(d_normal * unit_bn, axis=0)]))
    totals = jnp.pad(canonical(*sums), ((0, 6), (0, 0)))
    totals = halves(sum_everywhere(totals, 2)[0:2])
    total_rows = row_count * lax.axis_size("dp") * lax.axis_size("tensor")
    d_normed = 0.0
    grads_glu, grads_b, grads_depth = [], [], []
    for half in range(2):
        value, gate_sig, blocks, unit_bn, _, bn_inv, _ = kept[half]
        d_mixed = (
            bn_gains[half]
            * bn_inv
            * (
                d_normals[half]
                - totals[half][0] / total_rows
                - unit_bn * (totals[half][1] / total_rows)
            )
        )
        d_gated, grad_depth = depthwise_back(
            d_mixed.reshape(blocks.shape), blocks, depth_weights[half]
        )
        d_gated = d_gated.reshape(d_mixed.shape)
        d_pres = (d_gated * gate_sig, d_gated * value * gate_sig * (1.0 - gate_sig))
        grads_b.append(jnp.stack([jnp.sum(d_pre, axis=0) for d_pre in d_pres]))
        lows = [d_pre.astype(jnp.bfloat16) for d_pre in d_pres]
        grads_glu.append(jnp.stack([contract_first(normed, low) for low in lows]))
        for k, low in enumerate(lows):
            d_normed = d_normed + contract_last(low, glu_weights[half][k])
        grads_depth.append(grad_depth)
    summed = sum_in_turn(pair_sum([grads_glu, grads_out_w]), turn)
    d_stream, grad_gain, grad_shift = norm_backward(d_normed, unit_rows, inv_std, gain_row)
    return (
        stream_grad + d_stream,
        summed,
        (grads_b, grads_depth),
        (jnp.sum(stream_grad, axis=0), grad_gain, grad_shift),
        totals[0],
    )


def shards(
    inputs,
    cotangent,
    norm_gain,
    norm_shift,
    ff_in_weight,
    ff_in_bias,
    ff_out_weight,
    ff_out_bias,
    qkv_weight,
    pos_weight,
    content_bias,
    position_bias,
    attn_out_weight,
    attn_out_bias,
    glu_weight,
    glu_bias,
    depth_weight,
    bn_gain,
    bn_shift,
    conv_out_weight,
    conv_out_bias,
):
    width = bn_gain.shape[0]
    ff_rows = ff_in_bias.shape[1] // width
    small = jnp.concatenate(
        [
            ff_in_bias.reshape(2 * ff_rows, width),
            content_bias[None],
            position_bias[None],
            glu_bias,
            bn_gain[None],
            bn_shift[None],
            depth_weight,
        ],
        axis=0,
    )
    other = swap(small)
    at = 2 * ff_rows
    ff_in_biases = [
        (ff_in_bias[f], other[f * ff_rows : (f + 1) * ff_rows].reshape(-1)) for f in range(2)
    ]
    content = (content_bias, other[at])
    position = (position_bias, other[at + 1])
    glu_biases = (glu_bias, other[at + 2 : at + 4])
    bn_gains = (bn_gain, other[at + 4])
    bn_shifts = (bn_shift, other[at + 5])
    depth_weights = (depth_weight, other[at + 6 :])

    other_in, other_out = swap(ff_in_weight), swap(ff_out_weight)
    ff_in = [(ff_in_weight[f], other_in[f]) for f in range(2)]
    ff_out = [(ff_out_weight[f], other_out[f]) for f in range(2)]
    qkv = (qkv_weight, swap(qkv_weight))
    pos = (pos_weight, swap(pos_weight))
    attn_out = (attn_out_weight, swap(attn_out_weight))
    glu = (glu_weight, swap(glu_weight))
    conv_out = (conv_out_weight, swap(conv_out_weight))

    stream = inputs.astype(jnp.float32)
    stream, first_saved = ff_forward(
        stream, norm_gain[0], norm_shift[0], ff_in[0], ff_in_biases[0], ff_out[0], ff_out_bias[0]
    )
    stream, attn_saved = attn_forward(
        stream, norm_gain[1], norm_shift[1], qkv, pos, content, position, attn_out, attn_out_bias
    )
    stream, conv_saved = conv_forward(
        stream,
        norm_gain[2],
        norm_shift[2],
        glu,
        glu_biases,
        depth_weights,
        bn_gains,
        bn_shifts,
        conv_out,
        conv_out_bias,
    )
    stream, second_saved = ff_forward(
        stream, norm_gain[3], norm_shift[3], ff_in[1], ff_in_biases[1], ff_out[1], ff_out_bias[1]
    )
    result, final_unit, final_inv = norm_forward(stream, norm_gain[4], norm_shift[4])
    grad, final_gain, final_shift = norm_backward(cotangent, final_unit, final_inv, norm_gain[4])
    grad, second_sum, second_bias, second_rows = ff_backward(
        grad, second_saved, norm_gain[3], ff_in[1], ff_out[1], 0
    )
    grad, conv_sum, conv_small, conv_rows, bn_totals = conv_backward(
        grad, conv_saved, norm_gain[2], glu, depth_weights, bn_gains, conv_out, 1
    )
    grad, attn_sum, attn_small, attn_rows = attn_backward(
        grad, attn_saved, norm_gain[1], qkv, attn_out, 2, second_sum
    )
    grad, first_sum, first_bias, first_rows = ff_backward(
        grad, first_saved, norm_gain[0], ff_in[0], ff_out[0], 3
    )

    shared = jnp.stack(
        [first_rows[1], attn_rows[1], conv_rows[1], second_rows[1], final_gain]
        + [first_rows[2], attn_rows[2], conv_rows[2], second_rows[2], final_shift]
        + [first_rows[0], second_rows[0], attn_rows[0], conv_rows[0]]
    )
    split = [
        jnp.concatenate(
            [
                first_bias[half].reshape(ff_rows, width),
                second_bias[half].reshape(ff_rows, width),
                attn_small[half],
                conv_small[0][half],
                conv_small[1][half],
            ],
            axis=0,
        )
        for half in range(2)
    ]
    packed = jnp.concatenate([shared, canonical(*split)], axis=0)
    rows = packed.shape[0]
    packed = jnp.pad(packed, ((0, -rows % 8), (0, 0)))
    packed = sum_everywhere(packed, 3)
    own = halves(packed[14:rows])[0]
    return (
        result,
        grad,
        packed[0:5],
        packed[5:10],
        wide(jnp.stack([first_sum[0], second_sum[0]])),
        own[0 : 2 * ff_rows].reshape(2, ff_rows * width),
        wide(jnp.stack([first_sum[1], second_sum[1]])),
        packed[10:12],
        wide(attn_sum[0]),
        wide(attn_sum[1]),
        own[2 * ff_rows],
        own[2 * ff_rows + 1],
        wide(attn_sum[2]),
        packed[12],
        wide(conv_sum[0]),
        own[2 * ff_rows + 2 : 2 * ff_rows + 4],
        own[2 * ff_rows + 4 :],
        bn_totals[1],
        bn_totals[0],
        wide(conv_sum[1]),
        packed[13],
    )


def solution(mesh):
    in_specs = (
        P(("dp", "tensor"), None),
        P(("dp", "tensor"), None),
        P(),
        P(),
        P(None, None, "tensor"),
        P(None, "tensor"),
        P(None, "tensor", None),
        P(),
        P(None, None, "tensor"),
        P(None, "tensor"),
        P("tensor"),
        P("tensor"),
        P("tensor", None),
        P(),
        P(None, None, "tensor"),
        P(None, "tensor"),
        P(None, "tensor"),
        P("tensor"),
        P("tensor"),
        P("tensor", None),
        P(),
    )
    out_specs = (
        P(("dp", "tensor"), None),
        P(("dp", "tensor"), None),
        P(),
        P(),
        P(None, None, "tensor"),
        P(None, "tensor"),
        P(None, "tensor", None),
        P(),
        P(None, None, "tensor"),
        P(None, "tensor"),
        P("tensor"),
        P("tensor"),
        P("tensor", None),
        P(),
        P(None, None, "tensor"),
        P(None, "tensor"),
        P(None, "tensor"),
        P("tensor"),
        P("tensor"),
        P("tensor", None),
        P(),
    )
    return jax.shard_map(shards, mesh=mesh, in_specs=in_specs, out_specs=out_specs, check_vma=False)
```
